32 devices in a mesh: space: 16 (over z, x, core), snap: 2 (over y).
Axes of the slice: x: 2, y: 2, z: 4, core: 2. Of those that a mesh axis runs over, the one named last changes fastest.
Arguments:
- snapshots: bfloat16 [65536, 512], P('space', 'snap'), may hold values from -6 to 6
- basis: bfloat16 [65536, 64], P('space'), may hold values from -0.0234375 to 0.0234375
Outputs:
- normal: float32 [2144, 2144], P('snap')
- rhs: float32 [2144, 64], P('snap')
The draws below stay inside these ranges and needn't reach their ends.
All inputs are finite; a program needn't handle non-finite values.
Results may differ from the reference program's by a relative error of at most 0.0034.
Values sent between devices are 32-bit elements; how exact they have to be, the bound alone decides.
A program may use at most 64 MiB of HBM per device.

```python
import jax
import jax.numpy as jnp
import numpy as np

R = 64
NSPACE = 65536
NT = 512


def shard_levels(stream_key, extent, cuts, smallest, high):
    loudness, own = 1.0, jax.random.fold_in(stream_key, 6)
    for dim, blocks in cuts:
        draws = jnp.exp(jax.random.uniform(jax.random.fold_in(own, dim), (blocks,), jnp.float32, smallest / len(cuts), high / len(cuts)))
        loudness = loudness * jnp.repeat(draws, extent[dim] // blocks).reshape([-1 if axis == dim else 1 for axis in range(len(extent))])
    return loudness


def normal_values(rng, dims, deviation, limit, cuts=(), kind=jnp.bfloat16):
    result = deviation * jax.random.normal(rng, dims, jnp.float32)
    if cuts:
        result = result * shard_levels(rng, dims, cuts, -0.22, 0.18)
    return jnp.clip(result, -limit, limit).astype(kind)


def setup_inputs(seed: int = 0) -> dict:
    keys = jax.random.split(jax.random.key(seed), 3)
    snapshots = normal_values(keys[0], (NSPACE, NT), 1.0, 6.0, ((0, 16), (1, 2)))
    basis = normal_values(keys[1], (NSPACE, R), NSPACE ** -0.5, 0.0234375, ((0, 16),))
    return dict(snapshots=snapshots, basis=basis)


def make_features(states):
    upper_rows, upper_cols = np.triu_indices(R)
    quad = states[upper_rows, :] * states[upper_cols, :]
    return jnp.concatenate([states, quad], axis=0).T.astype(jnp.bfloat16)


def reference(snapshots, basis):
    states = jnp.dot(basis.T, snapshots, preferred_element_type=jnp.float32)
    targets = (jnp.roll(states, -1, axis=1) - states).T.astype(jnp.bfloat16)
    features = make_features(states)
    normal = jnp.dot(features.T, features, preferred_element_type=jnp.float32) / NT
    rhs = jnp.dot(features.T, targets, preferred_element_type=jnp.float32) / NT
    return normal, rhs
```

```python
import functools

import jax
import jax.numpy as jnp
import numpy as np
from jax import lax
from jax.experimental import pallas as pl
from jax.experimental.pallas import tpu as pltpu
from jax.sharding import PartitionSpec as P

MESH = pl.DeviceIdType.MESH
SUB, LANE = 8, 128
LOADS = 4


def states_kernel(n, m, snaps_hbm, basis_hbm, out_ref, snaps, basis, part, recv, gath, load_sem, sems):
    me, grp = lax.axis_index("space"), lax.axis_index("snap")
    peers = [(dp, ds) for ds in range(m) for dp in range(n) if dp or ds]

    step = snaps.shape[0] // LOADS
    loads = []
    for k in range(LOADS):
        rows = pl.ds(k * step, step)
        loads.append(
            (
                pltpu.make_async_copy(snaps_hbm.at[rows], snaps.at[rows], load_sem.at[0, k]),
                pltpu.make_async_copy(basis_hbm.at[:, rows], basis.at[:, rows], load_sem.at[1, k]),
            )
        )
        for load in loads[-1]:
            load.start()

    def device(dp, ds):
        return (lax.rem(me + dp, n), lax.rem(grp + ds, m))

    barrier = pltpu.get_barrier_semaphore()
    for dp, ds in peers:
        pl.semaphore_signal(barrier, inc=1, device_id=device(dp, ds), device_id_type=MESH)

    total = None
    for k in range(LOADS):
        for load in loads[k]:
            load.wait()
        piece = jnp.dot(
            basis[:, k * step : (k + 1) * step],
            snaps[k * step : (k + 1) * step, :],
            preferred_element_type=jnp.float32,
        )
        total = piece if total is None else total + piece
    rank, width = total.shape
    wide = width // LANE
    for r in range(rank // SUB):
        for q in range(wide):
            part[r * wide + q] = total[r * SUB : (r + 1) * SUB, q * LANE : (q + 1) * LANE]

    pl.semaphore_wait(barrier, len(peers))

    for dp in range(1, n):
        to = device(dp, 0)
        pltpu.make_async_remote_copy(
            src_ref=part.at[to[0]],
            dst_ref=recv.at[dp - 1],
            send_sem=sems.at[0],
            recv_sem=sems.at[1],
            device_id=to,
            device_id_type=MESH,
        ).start()
    pltpu.make_async_copy(recv, recv, sems.at[1]).wait()
    tile = part[me]
    for dp in range(1, n):
        tile = tile + recv[dp - 1]
    slot = grp * n + me
    gath[slot] = tile

    for dp, ds in peers:
        pltpu.make_async_remote_copy(
            src_ref=gath.at[slot],
            dst_ref=gath.at[slot],
            send_sem=sems.at[2],
            recv_sem=sems.at[3],
            device_id=device(dp, ds),
            device_id_type=MESH,
        ).start()
    others = gath.at[pl.ds(0, len(peers))]
    pltpu.make_async_copy(others, others, sems.at[3]).wait()
    for s in range(m):
        for r in range(rank // SUB):
            for q in range(wide):
                out_ref[r * SUB : (r + 1) * SUB, s * width + q * LANE : s * width + (q + 1) * LANE] = (
                    gath[s * n + r * wide + q]
                )
    pltpu.make_async_copy(recv, recv, sems.at[0]).wait()
    pltpu.make_async_copy(others, others, sems.at[2]).wait()


def all_states(snapshots, basis):
    n, m = lax.axis_size("space"), lax.axis_size("snap")
    rows, width = snapshots.shape
    rank = basis.shape[1]
    if n * SUB * LANE != rank * width:
        partial_value = lax.dot_general(
            basis, snapshots, (((0,), (0,)), ((), ())), preferred_element_type=jnp.float32
        )
        return lax.all_gather(lax.psum(partial_value, "space"), "snap", axis=1, tiled=True)
    return pl.pallas_call(
        functools.partial(states_kernel, n, m),
        out_shape=jax.ShapeDtypeStruct((rank, width * m), jnp.float32),
        in_specs=[pl.BlockSpec(memory_space=pl.ANY)] * 2,
        out_specs=pl.BlockSpec(memory_space=pltpu.VMEM),
        scratch_shapes=[
            pltpu.VMEM((rows, width), jnp.bfloat16),
            pltpu.VMEM((rank, rows), jnp.bfloat16),
            pltpu.VMEM((n, SUB, LANE), jnp.float32),
            pltpu.VMEM((n - 1, SUB, LANE), jnp.float32),
            pltpu.VMEM((n * m, SUB, LANE), jnp.float32),
            pltpu.SemaphoreType.DMA((2, LOADS)),
            pltpu.SemaphoreType.DMA((4,)),
        ],
        compiler_params=pltpu.CompilerParams(
            collective_id=0, has_side_effects=True, vmem_limit_bytes=32 * 2**20
        ),
        name="states",
    )(snapshots, basis.T)


COLS = 256


def normal_kernel(m, states_ref, normal_hbm, rhs_ref, quad, feats, normal, sems):
    rank, snaps = states_ref.shape
    width = rank + rank * (rank + 1) // 2
    rows = width // m
    states = states_ref[...]

    for a in range(rank - 1, -1, -1):
        lead = a % SUB
        start = rank + a * rank - a * (a - 1) // 2
        quad[start - lead : start - a + rank, :] = states[a - lead :, :] * states[a : a + 1, :]
    quad[:rank, :] = states
    feats[...] = quad[...].astype(jnp.bfloat16)

    scale = 1.0 / snaps
    mine = pl.multiple_of(lax.axis_index("snap") * rows, 16)
    dims = (((1,), (1,)), ((), ()))
    copies = []
    for j in range(0, width, COLS):
        cols = min(COLS, width - j)
        normal[:, j : j + cols] = (
            lax.dot_general(
                feats[pl.ds(mine, rows), :],
                feats[j : j + cols, :],
                dims,
                preferred_element_type=jnp.float32,
            )
            * scale
        )
        copies.append(
            pltpu.make_async_copy(
                normal.at[:, j : j + cols], normal_hbm.at[:, j : j + cols], sems.at[j // COLS]
            )
        )
        copies[-1].start()
    ahead = jnp.concatenate([states[:, 1:], states[:, :1]], axis=1)
    targets = (ahead - states).astype(jnp.bfloat16)
    rhs_ref[...] = (
        lax.dot_general(
            targets, feats[pl.ds(mine, rows), :], dims, preferred_element_type=jnp.float32
        )
        * scale
    )
    for copy in copies:
        copy.wait()


def row_block(states):
    rank, snaps = states.shape
    m = lax.axis_size("snap")
    width = rank + rank * (rank + 1) // 2
    rows = width // m
    if rows % 16 == 0:
        normal, rhs = pl.pallas_call(
            functools.partial(normal_kernel, m),
            out_shape=(
                jax.ShapeDtypeStruct((rows, width), jnp.float32),
                jax.ShapeDtypeStruct((rank, rows), jnp.float32),
            ),
            in_specs=[pl.BlockSpec(memory_space=pltpu.VMEM)],
            out_specs=(
                pl.BlockSpec(memory_space=pl.ANY),
                pl.BlockSpec(memory_space=pltpu.VMEM),
            ),
            scratch_shapes=[
                pltpu.VMEM((width, snaps), jnp.float32),
                pltpu.VMEM((width, snaps), jnp.bfloat16),
                pltpu.VMEM((rows, width), jnp.float32),
                pltpu.SemaphoreType.DMA((-(-width // COLS),)),
            ],
            compiler_params=pltpu.CompilerParams(vmem_limit_bytes=40 * 2**20),
            name="normal",
        )(states)
        return normal, rhs.T
    upper_rows, upper_cols = np.triu_indices(rank)
    quad = states[upper_rows, :] * states[upper_cols, :]
    features = jnp.concatenate([states, quad], axis=0).T.astype(jnp.bfloat16)
    targets = (jnp.roll(states, -1, axis=1) - states).T.astype(jnp.bfloat16)
    chosen = lax.dynamic_slice_in_dim(features, lax.axis_index("snap") * rows, rows, 1)
    dims = (((0,), (0,)), ((), ()))
    normal = lax.dot_general(chosen, features, dims, preferred_element_type=jnp.float32) / snaps
    rhs = lax.dot_general(chosen, targets, dims, preferred_element_type=jnp.float32) / snaps
    return normal, rhs


def per_device(snapshots, basis):
    return row_block(all_states(snapshots, basis))


def solution(mesh):
    return jax.shard_map(
        per_device,
        mesh=mesh,
        in_specs=(P("space", "snap"), P("space", None)),
        out_specs=(P("snap", None), P("snap", None)),
        check_vma=False,
    )
```

```python
import functools

import jax
import jax.numpy as jnp
import numpy as np
from jax import lax
from jax.experimental import pallas as pl
from jax.experimental.pallas import tpu as pltpu
from jax.sharding import PartitionSpec as P

MESH = pl.DeviceIdType.MESH
SUB, LANE = 8, 128
LOADS = 4
LIMIT = 107 * 2**19


def far_first(n):
    return sorted(range(1, n), key=lambda d: (-min(d, n - d), d))


def states_kernel(n, m, snaps_hbm, basis_hbm, out_ref, snaps, basis, part, recv, gath, load_sem, sems):
    me, grp = lax.axis_index("space"), lax.axis_index("snap")
    peers = [(dp, ds) for ds in range(m) for dp in far_first(n) + [0] if dp or ds]

    step = snaps.shape[0] // LOADS
    loads = []
    for k in range(LOADS):
        rows = pl.ds(k * step, step)
        loads.append(
            (
                pltpu.make_async_copy(snaps_hbm.at[rows], snaps.at[rows], load_sem.at[0, k]),
                pltpu.make_async_copy(basis_hbm.at[:, rows], basis.at[:, rows], load_sem.at[1, k]),
            )
        )
        for load in loads[-1]:
            load.start()

    def device(dp, ds):
        return (lax.rem(me + dp, n), lax.rem(grp + ds, m))

    barrier = pltpu.get_barrier_semaphore()
    for dp, ds in peers:
        pl.semaphore_signal(barrier, inc=1, device_id=device(dp, ds), device_id_type=MESH)

    total = None
    for k in range(LOADS):
        for load in loads[k]:
            load.wait()
        piece = jnp.dot(
            basis[:, k * step : (k + 1) * step],
            snaps[k * step : (k + 1) * step, :],
            preferred_element_type=jnp.float32,
        )
        total = piece if total is None else total + piece
    rank, width = total.shape
    wide = width // LANE
    for r in range(rank // SUB):
        for q in range(wide):
            part[r * wide + q] = total[r * SUB : (r + 1) * SUB, q * LANE : (q + 1) * LANE]

    pl.semaphore_wait(barrier, len(peers))

    for dp in far_first(n):
        to = device(dp, 0)
        pltpu.make_async_remote_copy(
            src_ref=part.at[to[0]],
            dst_ref=recv.at[dp - 1],
            send_sem=sems.at[0],
            recv_sem=sems.at[1],
            device_id=to,
            device_id_type=MESH,
        ).start()
    pltpu.make_async_copy(recv, recv, sems.at[1]).wait()
    tile = part[me]
    for dp in range(1, n):
        tile = tile + recv[dp - 1]
    slot = grp * n + me
    gath[slot] = tile

    for dp, ds in peers:
        pltpu.make_async_remote_copy(
            src_ref=gath.at[slot],
            dst_ref=gath.at[slot],
            send_sem=sems.at[2],
            recv_sem=sems.at[3],
            device_id=device(dp, ds),
            device_id_type=MESH,
        ).start()
    others = gath.at[pl.ds(0, len(peers))]
    pltpu.make_async_copy(others, others, sems.at[3]).wait()
    for s in range(m):
        for r in range(rank // SUB):
            for q in range(wide):
                out_ref[r * SUB : (r + 1) * SUB, s * width + q * LANE : s * width + (q + 1) * LANE] = (
                    gath[s * n + r * wide + q]
                )
    pltpu.make_async_copy(recv, recv, sems.at[0]).wait()
    pltpu.make_async_copy(others, others, sems.at[2]).wait()


def all_states(snapshots, basis):
    n, m = lax.axis_size("space"), lax.axis_size("snap")
    rows, width = snapshots.shape
    rank = basis.shape[1]
    if n * SUB * LANE != rank * width:
        partial_value = lax.dot_general(
            basis, snapshots, (((0,), (0,)), ((), ())), preferred_element_type=jnp.float32
        )
        return lax.all_gather(lax.psum(partial_value, "space"), "snap", axis=1, tiled=True)
    return pl.pallas_call(
        functools.partial(states_kernel, n, m),
        out_shape=jax.ShapeDtypeStruct((rank, width * m), jnp.float32),
        in_specs=[pl.BlockSpec(memory_space=pltpu.HBM)] * 2,
        out_specs=pl.BlockSpec(memory_space=pltpu.VMEM),
        scratch_shapes=[
            pltpu.VMEM((rows, width), jnp.bfloat16),
            pltpu.VMEM((rank, rows), jnp.bfloat16),
            pltpu.VMEM((n, SUB, LANE), jnp.float32),
            pltpu.VMEM((n - 1, SUB, LANE), jnp.float32),
            pltpu.VMEM((n * m, SUB, LANE), jnp.float32),
            pltpu.SemaphoreType.DMA((2, LOADS)),
            pltpu.SemaphoreType.DMA((4,)),
        ],
        compiler_params=pltpu.CompilerParams(
            collective_id=0, has_side_effects=True, vmem_limit_bytes=LIMIT
        ),
        name="states",
    )(snapshots, basis.T)


COLS = 256


def normal_kernel(m, states_ref, normal_hbm, rhs_ref, quad, feats, normal, sems):
    rank, snaps = states_ref.shape
    width = rank + rank * (rank + 1) // 2
    rows = width // m
    states = states_ref[...]

    for a in range(rank - 1, -1, -1):
        lead = a % SUB
        start = rank + a * rank - a * (a - 1) // 2
        quad[start - lead : start - a + rank, :] = states[a - lead :, :] * states[a : a + 1, :]
    quad[:rank, :] = states
    feats[...] = quad[...].astype(jnp.bfloat16)

    scale = 1.0 / snaps
    mine = pl.multiple_of(lax.axis_index("snap") * rows, 16)
    dims = (((1,), (1,)), ((), ()))
    copies = []
    for j in range(0, width, COLS):
        cols = min(COLS, width - j)
        normal[:, j : j + cols] = (
            lax.dot_general(
                feats[pl.ds(mine, rows), :],
                feats[j : j + cols, :],
                dims,
                preferred_element_type=jnp.float32,
            )
            * scale
        )
        copies.append(
            pltpu.make_async_copy(
                normal.at[:, j : j + cols], normal_hbm.at[:, j : j + cols], sems.at[j // COLS]
            )
        )
        copies[-1].start()
    ahead = jnp.concatenate([states[:, 1:], states[:, :1]], axis=1)
    targets = (ahead - states).astype(jnp.bfloat16)
    rhs_ref[...] = (
        lax.dot_general(
            targets, feats[pl.ds(mine, rows), :], dims, preferred_element_type=jnp.float32
        )
        * scale
    )
    for copy in copies:
        copy.wait()


def row_block(states):
    rank, snaps = states.shape
    m = lax.axis_size("snap")
    width = rank + rank * (rank + 1) // 2
    rows = width // m
    if rows % 16 == 0:
        normal, rhs = pl.pallas_call(
            functools.partial(normal_kernel, m),
            out_shape=(
                jax.ShapeDtypeStruct((rows, width), jnp.float32),
                jax.ShapeDtypeStruct((rank, rows), jnp.float32),
            ),
            in_specs=[pl.BlockSpec(memory_space=pltpu.VMEM)],
            out_specs=(
                pl.BlockSpec(memory_space=pl.ANY),
                pl.BlockSpec(memory_space=pltpu.VMEM),
            ),
            scratch_shapes=[
                pltpu.VMEM((width, snaps), jnp.float32),
                pltpu.VMEM((width, snaps), jnp.bfloat16),
                pltpu.VMEM((rows, width), jnp.float32),
                pltpu.SemaphoreType.DMA((-(-width // COLS),)),
            ],
            compiler_params=pltpu.CompilerParams(vmem_limit_bytes=40 * 2**20),
            name="normal",
        )(states)
        return normal, rhs.T
    upper_rows, upper_cols = np.triu_indices(rank)
    quad = states[upper_rows, :] * states[upper_cols, :]
    features = jnp.concatenate([states, quad], axis=0).T.astype(jnp.bfloat16)
    targets = (jnp.roll(states, -1, axis=1) - states).T.astype(jnp.bfloat16)
    chosen = lax.dynamic_slice_in_dim(features, lax.axis_index("snap") * rows, rows, 1)
    dims = (((0,), (0,)), ((), ()))
    normal = lax.dot_general(chosen, features, dims, preferred_element_type=jnp.float32) / snaps
    rhs = lax.dot_general(chosen, targets, dims, preferred_element_type=jnp.float32) / snaps
    return normal, rhs


def per_device(snapshots, basis):
    return row_block(all_states(snapshots, basis))


def solution(mesh):
    return jax.shard_map(
        per_device,
        mesh=mesh,
        in_specs=(P("space", "snap"), P("space", None)),
        out_specs=(P("snap", None), P("snap", None)),
        check_vma=False,
    )
```
